256 devices in a mesh: row: 8 (over x_hi, y), col: 16 (over x_lo, z), rep: 2 (over core).
Axes of the slice: x: 4 (x_hi: 2, x_lo: 2; x = x_hi * 2 + x_lo), y: 4, z: 8, core: 2. Of those that a mesh axis runs over, the one named last changes fastest.
Arguments:
- tokens: bfloat16 [6144, 12288], P(('rep', 'col'), 'row'), parts along dimension 0, may hold values from -6 to 6
- out_grad: bfloat16 [6144, 4096], P(('rep', 'row'), 'col'), parts along dimension 0, may hold values from -0.5 to 0.5
- weight: bfloat16 [24576, 4096], P(('rep', 'row'), 'col'), parts along dimension 0, may hold values from -0.0546875 to 0.0546875
- first_moment: float32 [24576, 4096], P(('rep', 'row'), 'col'), parts along dimension 0, may hold values from -6 to 6
- second_moment: float32 [24576, 4096], P(('rep', 'row'), 'col'), parts along dimension 0, may hold values from 0.5 to 8
Outputs:
- in_grad: bfloat16 [6144, 12288], P(('rep', 'col'), 'row'), parts along dimension 0
- new_weight: bfloat16 [24576, 4096], P(('rep', 'row'), 'col'), parts along dimension 0
- new_first: float32 [24576, 4096], P(('rep', 'row'), 'col'), parts along dimension 0
- new_second: float32 [24576, 4096], P(('rep', 'row'), 'col'), parts along dimension 0
The draws below stay inside these ranges and needn't reach their ends.
There are 2 independent parts, one for each index of `rep`. The reference program is written for one: setup_inputs(seed, part) draws one part's arguments, and reference() takes and returns one part's arrays. A program takes and returns all parts, laid end to end along the dimension named above; each array names one. Nothing has to cross between parts.
All inputs are finite; a program needn't handle non-finite values.
Results may differ from the reference program's by a relative error of at most 0.001.
Values may be sent and summed in bfloat16 or wider, within the bound.
A program may use at most 128 MiB of HBM per device.

```python
import math
import jax
import jax.numpy as jnp

D = 12288
SLAB = 4096
ADAM_STEP = 10
TOKENS = 3072


def block_scale(rng, shape, pieces, low, largest):
    factor_of, own = 1.0, jax.random.fold_in(rng, 6)
    for dim, blocks in pieces:
        draws = jnp.exp(jax.random.uniform(jax.random.fold_in(own, dim), (blocks,), jnp.float32, low / len(pieces), largest / len(pieces)))
        factor_of = factor_of * jnp.repeat(draws, shape[dim] // blocks).reshape([-1 if axis == dim else 1 for axis in range(len(shape))])
    return factor_of


def noise(rng, extent, width, most, shards=(), kind=jnp.bfloat16):
    loudness = block_scale(rng, extent, shards, -0.22, 0.18) if shards else 1.0
    drawn = jax.random.normal(rng, extent, jnp.float32) * width * loudness
    return jnp.minimum(jnp.maximum(drawn, -most), most).astype(kind)


def setup_inputs(seed: int = 0, part: int = 0) -> dict:
    seeds = jax.random.split(jax.random.key(seed), 6)
    part_keys = jax.random.split(jax.random.fold_in(seeds[5], part), 6)
    return {
        "tokens": noise(part_keys[0], (TOKENS, D), 1.0, 6.0, ((0, 16), (1, 8))),
        "out_grad": noise(part_keys[1], (TOKENS, SLAB), (2.0 / TOKENS ** 0.5), 0.5, ((0, 8), (1, 16))),
        "weight": noise(part_keys[2], (D, SLAB), D ** -0.5, 0.0546875, ((0, 8), (1, 16))),
        "first_moment": noise(part_keys[3], (D, SLAB), 1.0, 6.0, ((0, 8), (1, 16)), jnp.float32),
        "second_moment": jnp.clip(jnp.exp(math.log(8.0) - 2.7725887 * jax.random.uniform(part_keys[4], (D, SLAB), jnp.float32) ** block_scale(part_keys[4], (D, SLAB), ((0, 8), (1, 16)), -0.2, 0.2)), 0.5, 8.0),
    }


def reference(tokens, out_grad, weight, first_moment, second_moment):
    in_grad = jnp.dot(out_grad, weight.T, preferred_element_type=jnp.float32).astype(jnp.bfloat16)
    wgrad = jnp.dot(tokens.T, out_grad, preferred_element_type=jnp.float32)
    new_first = 0.9 * first_moment + 0.1 * wgrad
    new_second = 0.95 * second_moment + 0.05 * wgrad * wgrad
    first_hat = new_first / (1.0 - 0.9 ** ADAM_STEP)
    second_hat = new_second / (1.0 - 0.95 ** ADAM_STEP)
    old = weight.astype(jnp.float32)
    new_weight = (old - 0.001 * first_hat / (jnp.sqrt(second_hat) + 1e-08) - 0.0001 * old).astype(jnp.bfloat16)
    return (in_grad, new_weight, new_first, new_second)
```

```python
import functools

import jax
import jax.numpy as jnp
from jax import lax
from jax.experimental import pallas as pl
from jax.experimental.pallas import tpu as pltpu
from jax.sharding import PartitionSpec as P

ADAM_STEP = 10
MESH = pl.DeviceIdType.MESH
XH, XL, NY, NZ = 2, 2, 4, 8
CHUNK = 384


def kernel(
    tokens, og, weight, wgrad_out, in_grad_out,
    tk, wg, ogy, ogw, ogi, part, part_in, quota, quota_in, in_grad,
    ring_send, ring_recv, y_send, y_recv, w_send, w_recv, z_send, z_recv,
    h_send, h_recv, b_send, b_recv, x_send, x_recv, local,
):
    tb, d = tokens.shape
    ob, f = og.shape
    n_chunks = d // CHUNK
    n_items = 2 * n_chunks
    quarter = tb // NY
    half_t = NZ * tb

    r, c = lax.axis_index("row"), lax.axis_index("col")
    xh, y = r // NY, lax.rem(r, NY)
    xl, z = c // NZ, lax.rem(c, NZ)

    def dev(xh_, y_, xl_, z_):
        return {"row": xh_ * NY + y_, "col": xl_ * NZ + z_}

    def remote(src, dst, s, rcv, to):
        return pltpu.make_async_remote_copy(
            src_ref=src, dst_ref=dst, send_sem=s, recv_sem=rcv, device_id=to, device_id_type=MESH
        )

    own = [
        pltpu.make_async_copy(tokens, tk.at[z], local.at[0]),
        pltpu.make_async_copy(weight, wg.at[z], local.at[1]),
        pltpu.make_async_copy(og, ogy.at[pl.ds(y * ob, ob)], local.at[2]),
    ]
    for o in own:
        o.start()

    barrier = pltpu.get_barrier_semaphore()
    peers = [dev(xh, lax.rem(y + k, NY), xl, z) for k in range(1, NY)]
    peers += [dev(xh, y, xl, lax.rem(z + k, NZ)) for k in range(1, NZ)]
    peers += [dev(1 - xh, y, xl, z), dev(xh, y, 1 - xl, z), dev(1 - xh, y, 1 - xl, z)]
    for p in peers:
        pl.semaphore_signal(barrier, inc=1, device_id=p, device_id_type=MESH)
    pl.semaphore_wait(barrier, len(peers))

    y_copies = []
    for k in range(1, NY):
        y_copies.append(
            remote(og, ogy.at[pl.ds(y * ob, ob)], y_send.at[k - 1], y_recv.at[k - 1], dev(xh, lax.rem(y + k, NY), xl, z))
        )
        y_copies[-1].start()

    right, left = lax.rem(z + 1, NZ), lax.rem(z + NZ - 1, NZ)

    def piece(item, src_z, half):
        if item < n_chunks:
            rows = pl.ds(0, tb) if half is None else pl.ds(half * (tb // 2), tb // 2)
            return tk.at[src_z, rows, pl.ds(item * CHUNK, CHUNK)]
        d0 = (item - n_chunks) * CHUNK
        rows = pl.ds(d0, CHUNK) if half is None else pl.ds(d0 + half * (CHUNK // 2), CHUNK // 2)
        return wg.at[src_z, rows]

    def ring_copy(item, way, hop):
        half = way if hop == NZ // 2 else None
        step = hop - 1
        src_z = lax.rem(z + (NZ - step if way == 0 else step), NZ)
        ref = piece(item, src_z, half)
        if hop == 1:
            if item < n_chunks:
                src = tokens.at[:, pl.ds(item * CHUNK, CHUNK)]
            else:
                src = weight.at[pl.ds((item - n_chunks) * CHUNK, CHUNK)]
        else:
            src = ref
        to = right if way == 0 else left
        return remote(src, ref, ring_send.at[item, way, step], ring_recv.at[item, way, step], dev(xh, y, xl, to))

    def ring_arrival(item, way, hop):
        half = way if hop == NZ // 2 else None
        src_z = lax.rem(z + (NZ - hop if way == 0 else hop), NZ)
        ref = piece(item, src_z, half)
        return remote(ref, ref, ring_send.at[item, way, hop - 1], ring_recv.at[item, way, hop - 1], dev(xh, y, xl, right))

    ring_copies = []

    def ring_start(item, hop):
        for way in (0, 1):
            copy = ring_copy(item, way, hop)
            copy.start()
            ring_copies.append(copy)

    same = xh == xl

    def w_copy(k):
        return remote(ogy, ogw.at[xl], w_send.at[k], w_recv.at[xl], dev(k, y, xh, z))

    def w_arrival(j):
        return remote(ogy, ogw.at[j], w_send.at[j], w_recv.at[j], dev(xh, y, 1 - xl, z))

    def w_local():
        return pltpu.make_async_copy(ogy, ogw.at[xl], local.at[3])

    def w_start():
        for k in range(XH):
            @pl.when(jnp.logical_or(k != xh, jnp.logical_not(same)))
            def _():
                w_copy(k).start()

        @pl.when(same)
        def _():
            w_local().start()

    def w_wait():
        for j in range(XL):
            @pl.when(jnp.logical_or(j != xl, jnp.logical_not(same)))
            def _():
                w_arrival(j).wait_recv()

        @pl.when(same)
        def _():
            w_local().wait()

    def w_wait_send():
        for k in range(XH):
            @pl.when(jnp.logical_or(k != xh, jnp.logical_not(same)))
            def _():
                w_copy(k).wait_send()

    def strip(h, y_):
        return ogi.at[:, h, pl.ds(y_ * quarter, quarter)]

    def z_copy(k):
        to = lax.rem(z + k, NZ)
        src = ogy.at[pl.ds(to * tb + y * quarter, quarter)]
        return remote(src, ogi.at[z, xh, pl.ds(y * quarter, quarter)], z_send.at[k - 1], z_recv.at[k - 1], dev(xh, y, xl, to))

    def z_arrival(k):
        at = lax.rem(z + NZ - k, NZ)
        ref = ogi.at[at, xh, pl.ds(y * quarter, quarter)]
        return remote(ref, ref, z_send.at[k - 1], z_recv.at[k - 1], dev(xh, y, xl, at))

    z_local = pltpu.make_async_copy(
        ogy.at[pl.ds(z * tb + y * quarter, quarter)], ogi.at[z, xh, pl.ds(y * quarter, quarter)], local.at[4]
    )
    h_copy = remote(strip(xh, y), strip(xh, y), h_send, h_recv, dev(1 - xh, y, xl, z))
    h_arrival = remote(strip(1 - xh, y), strip(1 - xh, y), h_send, h_recv, dev(1 - xh, y, xl, z))

    def b_copy(which, k):
        h = xh if which == 0 else 1 - xh
        return remote(strip(h, y), strip(h, y), b_send.at[which, k - 1], b_recv.at[which, k - 1], dev(xh, lax.rem(y + k, NY), xl, z))

    def b_arrival(which, k):
        h = xh if which == 0 else 1 - xh
        ref = strip(h, lax.rem(y + NY - k, NY))
        return remote(ref, ref, b_send.at[which, k - 1], b_recv.at[which, k - 1], dev(xh, lax.rem(y + k, NY), xl, z))

    def x_copy(item):
        d0 = (item % n_chunks) * CHUNK
        if item < n_chunks:
            src, dst = part.at[1 - xl, pl.ds(d0, CHUNK)], part_in.at[pl.ds(d0, CHUNK)]
        else:
            src, dst = quota.at[1 - xl, :, pl.ds(d0, CHUNK)], quota_in.at[:, pl.ds(d0, CHUNK)]
        return remote(src, dst, x_send.at[item], x_recv.at[item], dev(xh, y, 1 - xl, z))

    def multiply(item):
        d0 = (item % n_chunks) * CHUNK
        if item < n_chunks:
            def body(i, _):
                cols = pl.ds(pl.multiple_of(d0 + i * 128, 128), 128)
                a = tk[:, :, cols].reshape(half_t, 128)
                for k in range(XL):
                    part[k, cols] = lax.dot_general(
                        a, ogw[k], (((0,), (0,)), ((), ())), preferred_element_type=jnp.float32
                    )
                return 0

            lax.fori_loop(0, CHUNK // 128, body, 0)
        else:
            def body(i, _):
                k = i
                total = jnp.zeros((tb, CHUNK), jnp.float32)
                for s in range(NZ):
                    total += lax.dot_general(
                        ogi[s, k], wg[s, pl.ds(d0, CHUNK)], (((1,), (1,)), ((), ())), preferred_element_type=jnp.float32
                    )
                quota[k, :, pl.ds(d0, CHUNK)] = total
                return 0

            lax.fori_loop(0, XL, body, 0)

    outs = []

    def finish(item):
        d0 = (item % n_chunks) * CHUNK
        x_copy(item).wait_recv()
        if item < n_chunks:
            part[xl, pl.ds(d0, CHUNK)] = part[xl, pl.ds(d0, CHUNK)] + part_in[pl.ds(d0, CHUNK)]
            out = pltpu.make_async_copy(part.at[xl, pl.ds(d0, CHUNK)], wgrad_out.at[pl.ds(d0, CHUNK)], local.at[5 + item])
        else:
            cols = pl.ds(d0, CHUNK)
            in_grad[:, cols] = (quota[xl, :, cols] + quota_in[:, cols]).astype(in_grad.dtype)
            out = pltpu.make_async_copy(in_grad.at[:, cols], in_grad_out.at[:, cols], local.at[5 + item])
        out.start()
        outs.append(out)

    hops = NZ // 2
    ring_start(0, 1)
    ring_start(1, 1)
    for step in range(n_items + hops - 1):
        for hop in range(hops, 0, -1):
            item = step - (hop - 1)
            if 0 <= item < n_items:
                for way in (0, 1):
                    ring_arrival(item, way, hop).wait_recv()
                if hop < hops:
                    ring_start(item, hop + 1)
        if step + 2 < n_items:
            ring_start(step + 2, 1)
        if step == 0:
            own[2].wait()
            for k in range(1, NY):
                src = ogy.at[pl.ds(lax.rem(y + NY - k, NY) * ob, ob)]
                remote(src, src, y_send.at[k - 1], y_recv.at[k - 1], dev(xh, lax.rem(y + k, NY), xl, z)).wait_recv()
            w_start()
            for k in range(1, NZ):
                z_copy(k).start()
            z_local.start()
        if step == 1:
            z_local.wait()
            for k in range(1, NZ):
                z_arrival(k).wait_recv()
            h_copy.start()
            for k in range(1, NY):
                b_copy(0, k).start()
        if step == 2:
            h_arrival.wait_recv()
            for k in range(1, NY):
                b_copy(1, k).start()
            own[0].wait()
            own[1].wait()
        done = step - (hops - 1)
        if done == 0:
            w_wait()
        if done == 2:
            for which in (0, 1):
                for k in range(1, NY):
                    b_arrival(which, k).wait_recv()
        if done >= 0:
            multiply(done)
            x_copy(done).start()
            if done >= 2:
                finish(done - 2)
    finish(n_items - 2)
    finish(n_items - 1)

    for copy in y_copies + ring_copies:
        copy.wait_send()
    w_wait_send()
    for k in range(1, NZ):
        z_copy(k).wait_send()
    h_copy.wait_send()
    for which in (0, 1):
        for k in range(1, NY):
            b_copy(which, k).wait_send()
    for item in range(n_items):
        x_copy(item).wait_send()
    for out in outs:
        out.wait()


def products(tokens, out_grad, weight):
    tb, d = tokens.shape
    ob, f = out_grad.shape
    n_items = 2 * (d // CHUNK)
    dma = pltpu.SemaphoreType.DMA
    flops = 4 * d * f * ob * XH * NY
    return pl.pallas_call(
        kernel,
        out_shape=(
            jax.ShapeDtypeStruct((d, f), jnp.float32),
            jax.ShapeDtypeStruct((tb, d), jnp.bfloat16),
        ),
        in_specs=[pl.BlockSpec(memory_space=pl.ANY)] * 3,
        out_specs=[pl.BlockSpec(memory_space=pl.ANY)] * 2,
        scratch_shapes=[
            pltpu.VMEM((NZ, tb, d), jnp.bfloat16),
            pltpu.VMEM((NZ, d, f), jnp.bfloat16),
            pltpu.VMEM((NY * ob, f), jnp.bfloat16),
            pltpu.VMEM((XL, NY * ob, f), jnp.bfloat16),
            pltpu.VMEM((NZ, XH, tb, f), jnp.bfloat16),
            pltpu.VMEM((XL, d, f), jnp.float32),
            pltpu.VMEM((d, f), jnp.float32),
            pltpu.VMEM((XL, tb, d), jnp.float32),
            pltpu.VMEM((tb, d), jnp.float32),
            pltpu.VMEM((tb, d), jnp.bfloat16),
            dma((n_items, 2, NZ // 2)),
            dma((n_items, 2, NZ // 2)),
            dma((NY - 1,)),
            dma((NY - 1,)),
            dma((XH,)),
            dma((XL,)),
            dma((NZ - 1,)),
            dma((NZ - 1,)),
            dma,
            dma,
            dma((2, NY - 1)),
            dma((2, NY - 1)),
            dma((n_items,)),
            dma((n_items,)),
            dma((5 + n_items,)),
        ],
        compiler_params=pltpu.CompilerParams(
            collective_id=0, has_side_effects=True, vmem_limit_bytes=48 * 2**20
        ),
        cost_estimate=pl.CostEstimate(flops=flops, bytes_accessed=8 * 2**20, transcendentals=0),
    )(tokens, out_grad, weight)


def per_device(tokens, out_grad, weight, first_moment, second_moment):
    wgrad, in_grad = products(tokens, out_grad, weight)
    new_first = 0.9 * first_moment + 0.1 * wgrad
    new_second = 0.95 * second_moment + 0.05 * wgrad * wgrad
    first_hat = new_first / (1.0 - 0.9**ADAM_STEP)
    second_hat = new_second / (1.0 - 0.95**ADAM_STEP)
    old = weight.astype(jnp.float32)
    new_weight = (old - 0.001 * first_hat / (jnp.sqrt(second_hat) + 1e-08) - 0.0001 * old).astype(
        jnp.bfloat16
    )
    return (in_grad, new_weight, new_first, new_second)


def solution(mesh):
    placed = (
        P(("rep", "col"), "row"),
        P(("rep", "row"), "col"),
        P(("rep", "row"), "col"),
        P(("rep", "row"), "col"),
        P(("rep", "row"), "col"),
    )
    return jax.shard_map(
        per_device,
        mesh=mesh,
        in_specs=placed,
        out_specs=(
            P(("rep", "col"), "row"),
            P(("rep", "row"), "col"),
            P(("rep", "row"), "col"),
            P(("rep", "row"), "col"),
        ),
        check_vma=False,
    )
```

```python
import functools

import jax
import jax.numpy as jnp
from jax import lax
from jax.experimental import pallas as pl
from jax.experimental.pallas import tpu as pltpu
from jax.sharding import PartitionSpec as P

ADAM_STEP = 10
MESH = pl.DeviceIdType.MESH
XH, XL, NY, NZ = 2, 2, 4, 8
LOOK = 4
TOKEN_CHUNKS = (384, 384, 384, 384)
WEIGHT_CHUNKS = (384, 384, 384, 256, 128)
LAST = 128
PACE = 1
DRAIN = 0
SETTLE = 2
STAGES = (0, 1, 2)


def chunks():
    items = []
    for widths in (TOKEN_CHUNKS, WEIGHT_CHUNKS):
        first = 0
        for width in widths:
            items.append((first, width))
            first += width
    return items


def parts_of(items):
    parts = [(item, first, width) for item, (first, width) in enumerate(items[:-1])]
    first, width = items[-1]
    return parts + [(len(items) - 1, first + at, LAST) for at in range(0, width, LAST)]


def kernel(
    tokens, og, weight, wgrad_out, in_grad_out,
    tk, wg, ogy, ogw, ogi, part, part_in, quota, quota_in, in_grad,
    ring_send, ring_recv, y_send, y_recv, w_send, w_recv, z_send, z_recv,
    h_send, h_recv, b_send, b_recv, x_send, x_recv, local,
):
    tb, d = tokens.shape
    ob, f = og.shape
    n_chunks, items = len(TOKEN_CHUNKS), chunks()
    n_items = len(items)
    prods = parts_of(items)
    quarter = tb // NY
    half_t = NZ * tb

    r, c = lax.axis_index("row"), lax.axis_index("col")
    xh, y = r // NY, lax.rem(r, NY)
    xl, z = c // NZ, lax.rem(c, NZ)

    def dev(xh_, y_, xl_, z_):
        return {"row": xh_ * NY + y_, "col": xl_ * NZ + z_}

    def remote(src, dst, s, rcv, to):
        return pltpu.make_async_remote_copy(
            src_ref=src, dst_ref=dst, send_sem=s, recv_sem=rcv, device_id=to, device_id_type=MESH
        )

    own = [
        pltpu.make_async_copy(tokens, tk.at[z], local.at[0]),
        pltpu.make_async_copy(weight, wg.at[z], local.at[1]),
        pltpu.make_async_copy(og, ogy.at[pl.ds(y * ob, ob)], local.at[2]),
    ]
    for o in own:
        o.start()

    barrier = pltpu.get_barrier_semaphore()
    peers = [dev(xh, lax.rem(y + k, NY), xl, z) for k in range(1, NY)]
    peers += [dev(xh, y, xl, lax.rem(z + k, NZ)) for k in range(1, NZ)]
    peers += [dev(1 - xh, y, xl, z), dev(xh, y, 1 - xl, z), dev(1 - xh, y, 1 - xl, z)]
    for p in peers:
        pl.semaphore_signal(barrier, inc=1, device_id=p, device_id_type=MESH)
    pl.semaphore_wait(barrier, len(peers))

    y_copies = []
    for k in range(1, NY):
        y_copies.append(
            remote(og, ogy.at[pl.ds(y * ob, ob)], y_send.at[k - 1], y_recv.at[k - 1], dev(xh, lax.rem(y + k, NY), xl, z))
        )
        y_copies[-1].start()

    right, left = lax.rem(z + 1, NZ), lax.rem(z + NZ - 1, NZ)

    def piece(item, src_z, half):
        d0, width = items[item]
        if item < n_chunks:
            rows = pl.ds(0, tb) if half is None else pl.ds(half * (tb // 2), tb // 2)
            return tk.at[src_z, rows, pl.ds(d0, width)]
        rows = pl.ds(d0, width) if half is None else pl.ds(d0 + half * (width // 2), width // 2)
        return wg.at[src_z, rows]

    def ring_copy(item, way, hop):
        half = way if hop == NZ // 2 else None
        step = hop - 1
        src_z = lax.rem(z + (NZ - step if way == 0 else step), NZ)
        ref = piece(item, src_z, half)
        src = ref
        to = right if way == 0 else left
        return remote(src, ref, ring_send.at[item, way, step], ring_recv.at[item, way, step], dev(xh, y, xl, to))

    def ring_arrival(item, way, hop):
        half = way if hop == NZ // 2 else None
        src_z = lax.rem(z + (NZ - hop if way == 0 else hop), NZ)
        ref = piece(item, src_z, half)
        return remote(ref, ref, ring_send.at[item, way, hop - 1], ring_recv.at[item, way, hop - 1], dev(xh, y, xl, right))

    own[0].wait()
    ring_copies = []

    def ring_start(item, hop, ways=(0, 1)):
        for way in ways:
            copy = ring_copy(item, way, hop)
            copy.start()
            ring_copies.append(copy)

    same = xh == xl

    def w_copy(k):
        return remote(ogy, ogw.at[xl], w_send.at[k], w_recv.at[xl], dev(k, y, xh, z))

    def w_arrival(j):
        return remote(ogy, ogw.at[j], w_send.at[j], w_recv.at[j], dev(xh, y, 1 - xl, z))

    def w_local():
        return pltpu.make_async_copy(ogy, ogw.at[xl], local.at[3])

    def w_start():
        for k in range(XH):
            @pl.when(jnp.logical_or(k != xh, jnp.logical_not(same)))
            def _():
                w_copy(k).start()

        @pl.when(same)
        def _():
            w_local().start()

    def w_wait():
        for j in range(XL):
            @pl.when(jnp.logical_or(j != xl, jnp.logical_not(same)))
            def _():
                w_arrival(j).wait_recv()

        @pl.when(same)
        def _():
            w_local().wait()

    def w_wait_send():
        for k in range(XH):
            @pl.when(jnp.logical_or(k != xh, jnp.logical_not(same)))
            def _():
                w_copy(k).wait_send()

    def strip(h, y_):
        return ogi.at[:, h, pl.ds(y_ * quarter, quarter)]

    def z_copy(k):
        to = lax.rem(z + k, NZ)
        src = ogy.at[pl.ds(to * tb + y * quarter, quarter)]
        return remote(src, ogi.at[z, xh, pl.ds(y * quarter, quarter)], z_send.at[k - 1], z_recv.at[k - 1], dev(xh, y, xl, to))

    def z_arrival(k):
        at = lax.rem(z + NZ - k, NZ)
        ref = ogi.at[at, xh, pl.ds(y * quarter, quarter)]
        return remote(ref, ref, z_send.at[k - 1], z_recv.at[k - 1], dev(xh, y, xl, at))

    z_local = pltpu.make_async_copy(
        ogy.at[pl.ds(z * tb + y * quarter, quarter)], ogi.at[z, xh, pl.ds(y * quarter, quarter)], local.at[4]
    )
    h_copy = remote(strip(xh, y), strip(xh, y), h_send, h_recv, dev(1 - xh, y, xl, z))
    h_arrival = remote(strip(1 - xh, y), strip(1 - xh, y), h_send, h_recv, dev(1 - xh, y, xl, z))

    def b_copy(which, k):
        h = xh if which == 0 else 1 - xh
        return remote(strip(h, y), strip(h, y), b_send.at[which, k - 1], b_recv.at[which, k - 1], dev(xh, lax.rem(y + k, NY), xl, z))

    def b_arrival(which, k):
        h = xh if which == 0 else 1 - xh
        ref = strip(h, lax.rem(y + NY - k, NY))
        return remote(ref, ref, b_send.at[which, k - 1], b_recv.at[which, k - 1], dev(xh, lax.rem(y + k, NY), xl, z))

    def x_copy(at):
        item, d0, width = prods[at]
        if item < n_chunks:
            src, dst = part.at[1 - xl, pl.ds(d0, width)], part_in.at[pl.ds(d0, width)]
        else:
            src, dst = quota.at[1 - xl, :, pl.ds(d0, width)], quota_in.at[:, pl.ds(d0, width)]
        return remote(src, dst, x_send.at[at], x_recv.at[at], dev(xh, y, 1 - xl, z))

    def multiply(at):
        item, d0, width = prods[at]
        if item < n_chunks:
            def body(i, _):
                cols = pl.ds(pl.multiple_of(d0 + i * 128, 128), 128)
                a = tk[:, :, cols].reshape(half_t, 128)
                for k in range(XL):
                    part[k, cols] = lax.dot_general(
                        a, ogw[k], (((0,), (0,)), ((), ())), preferred_element_type=jnp.float32
                    )
                return 0

            lax.fori_loop(0, width // 128, body, 0)
        else:
            def body(i, _):
                k = i
                total = jnp.zeros((tb, width), jnp.float32)
                for s in range(NZ):
                    total += lax.dot_general(
                        ogi[s, k], wg[s, pl.ds(d0, width)], (((1,), (1,)), ((), ())), preferred_element_type=jnp.float32
                    )
                quota[k, :, pl.ds(d0, width)] = total
                return 0

            lax.fori_loop(0, XL, body, 0)

    outs = []

    def finish(at):
        item, d0, width = prods[at]
        x_copy(at).wait_recv()
        if item < n_chunks:
            part[xl, pl.ds(d0, width)] = part[xl, pl.ds(d0, width)] + part_in[pl.ds(d0, width)]
            out = pltpu.make_async_copy(part.at[xl, pl.ds(d0, width)], wgrad_out.at[pl.ds(d0, width)], local.at[5 + at])
        else:
            cols = pl.ds(d0, width)
            in_grad[:, cols] = (quota[xl, :, cols] + quota_in[:, cols]).astype(in_grad.dtype)
            out = pltpu.make_async_copy(in_grad.at[:, cols], in_grad_out.at[:, cols], local.at[5 + at])
        out.start()
        outs.append(out)

    hops = NZ // 2
    waiting = []
    next_product = 0
    for item in range(LOOK):
        ring_start(item, 1)

    def due(item, hop):
        return min(item + PACE * (hop - 1), n_items - 1 + DRAIN + hop - 1)

    for step in range(due(n_items - 1, hops) + 1):
        for hop in range(hops, 0, -1):
            for item in [i for i in range(n_items) if due(i, hop) == step]:
                for way in (0, 1):
                    ring_arrival(item, way, hop).wait_recv()
                    if hop < hops:
                        ring_start(item, hop + 1, (way,))
        if step + LOOK < n_items:
            if step + LOOK == n_chunks:
                own[1].wait()
            ring_start(step + LOOK, 1)
        if step == STAGES[0]:
            own[2].wait()
            for k in range(1, NY):
                src = ogy.at[pl.ds(lax.rem(y + NY - k, NY) * ob, ob)]
                remote(src, src, y_send.at[k - 1], y_recv.at[k - 1], dev(xh, lax.rem(y + k, NY), xl, z)).wait_recv()
            w_start()
            for k in range(1, NZ):
                z_copy(k).start()
            z_local.start()
        if step == STAGES[1]:
            z_local.wait()
            for k in range(1, NZ):
                z_arrival(k).wait_recv()
            h_copy.start()
            for k in range(1, NY):
                b_copy(0, k).start()
        if step == STAGES[2]:
            h_arrival.wait_recv()
            for k in range(1, NY):
                b_copy(1, k).start()
        while next_product < len(prods) and due(prods[next_product][0], hops) <= step:
            if next_product == 0:
                w_wait()
            if next_product == n_chunks:
                for which in (0, 1):
                    for k in range(1, NY):
                        b_arrival(which, k).wait_recv()
            multiply(next_product)
            x_copy(next_product).start()
            waiting.append((step, next_product))
            next_product += 1
        while waiting and waiting[0][0] <= step - SETTLE:
            finish(waiting.pop(0)[1])
    for _, item in waiting:
        finish(item)

    for copy in y_copies + ring_copies:
        copy.wait_send()
    w_wait_send()
    for k in range(1, NZ):
        z_copy(k).wait_send()
    h_copy.wait_send()
    for which in (0, 1):
        for k in range(1, NY):
            b_copy(which, k).wait_send()
    for at in range(len(prods)):
        x_copy(at).wait_send()
    for out in outs:
        out.wait()


def products(tokens, out_grad, weight):
    tb, d = tokens.shape
    ob, f = out_grad.shape
    items = chunks()
    n_items, n_prods = len(items), len(parts_of(items))
    dma = pltpu.SemaphoreType.DMA
    flops = 4 * d * f * ob * XH * NY
    return pl.pallas_call(
        kernel,
        out_shape=(
            jax.ShapeDtypeStruct((d, f), jnp.float32),
            jax.ShapeDtypeStruct((tb, d), jnp.bfloat16),
        ),
        in_specs=[pl.BlockSpec(memory_space=pltpu.HBM)] * 3,
        out_specs=[pl.BlockSpec(memory_space=pl.ANY)] * 2,
        scratch_shapes=[
            pltpu.VMEM((NZ, tb, d), jnp.bfloat16),
            pltpu.VMEM((NZ, d, f), jnp.bfloat16),
            pltpu.VMEM((NY * ob, f), jnp.bfloat16),
            pltpu.VMEM((XL, NY * ob, f), jnp.bfloat16),
            pltpu.VMEM((NZ, XH, tb, f), jnp.bfloat16),
            pltpu.VMEM((XL, d, f), jnp.float32),
            pltpu.VMEM((d, f), jnp.float32),
            pltpu.VMEM((XL, tb, d), jnp.float32),
            pltpu.VMEM((tb, d), jnp.float32),
            pltpu.VMEM((tb, d), jnp.bfloat16),
            dma((n_items, 2, NZ // 2)),
            dma((n_items, 2, NZ // 2)),
            dma((NY - 1,)),
            dma((NY - 1,)),
            dma((XH,)),
            dma((XL,)),
            dma((NZ - 1,)),
            dma((NZ - 1,)),
            dma,
            dma,
            dma((2, NY - 1)),
            dma((2, NY - 1)),
            dma((n_prods,)),
            dma((n_prods,)),
            dma((5 + n_prods,)),
        ],
        compiler_params=pltpu.CompilerParams(
            collective_id=0, has_side_effects=True, vmem_limit_bytes=60 * 2**20
        ),
        cost_estimate=pl.CostEstimate(flops=flops, bytes_accessed=8 * 2**20, transcendentals=0),
    )(tokens, out_grad, weight)


def per_device(tokens, out_grad, weight, first_moment, second_moment):
    wgrad, in_grad = products(tokens, out_grad, weight)
    new_first = 0.9 * first_moment + 0.1 * wgrad
    new_second = 0.95 * second_moment + 0.05 * wgrad * wgrad
    first_hat = new_first / (1.0 - 0.9**ADAM_STEP)
    second_hat = new_second / (1.0 - 0.95**ADAM_STEP)
    old = weight.astype(jnp.float32)
    new_weight = (old - 0.001 * first_hat / (jnp.sqrt(second_hat) + 1e-08) - 0.0001 * old).astype(
        jnp.bfloat16
    )
    return (in_grad, new_weight, new_first, new_second)


def solution(mesh):
    placed = (
        P(("rep", "col"), "row"),
        P(("rep", "row"), "col"),
        P(("rep", "row"), "col"),
        P(("rep", "row"), "col"),
        P(("rep", "row"), "col"),
    )
    return jax.shard_map(
        per_device,
        mesh=mesh,
        in_specs=placed,
        out_specs=(
            P(("rep", "col"), "row"),
            P(("rep", "row"), "col"),
            P(("rep", "row"), "col"),
            P(("rep", "row"), "col"),
        ),
        check_vma=False,
    )
```

```python
import functools

import jax
import jax.numpy as jnp
from jax import lax
from jax.experimental import pallas as pl
from jax.experimental.pallas import tpu as pltpu
from jax.sharding import PartitionSpec as P

ADAM_STEP = 10
MESH = pl.DeviceIdType.MESH
XH, XL, NY, NZ = 2, 2, 4, 8
LOOK = 4
TOKEN_CHUNKS = (384, 384, 384, 384)
WEIGHT_CHUNKS = (384, 384, 384, 256, 128)
LAST = 128
PACE = 1
DRAIN = 0
SETTLE = 2
STAGES = (0, 1, 2)


def chunks():
    items = []
    for widths in (TOKEN_CHUNKS, WEIGHT_CHUNKS):
        first = 0
        for width in widths:
            items.append((first, width))
            first += width
    return items


def parts_of(items):
    parts = [(item, first, width) for item, (first, width) in enumerate(items[:-1])]
    first, width = items[-1]
    return parts + [(len(items) - 1, first + at, LAST) for at in range(0, width, LAST)]


def kernel(
    tokens, og, weight, wgrad_out, in_grad_out,
    tk, wg, ogy, ogw, ogi, part, part_in, quota, quota_in, in_grad,
    ring_send, ring_recv, y_send, y_recv, w_send, w_recv, v_send, v_recv, z_send, z_recv,
    h_send, h_recv, b_send, b_recv, x_send, x_recv, local,
):
    tb, d = tokens.shape
    ob, f = og.shape
    n_chunks, items = len(TOKEN_CHUNKS), chunks()
    n_items = len(items)
    prods = parts_of(items)
    quarter = tb // NY
    half_t = NZ * tb

    r, c = lax.axis_index("row"), lax.axis_index("col")
    xh, y = r // NY, lax.rem(r, NY)
    xl, z = c // NZ, lax.rem(c, NZ)

    def dev(xh_, y_, xl_, z_):
        return {"row": xh_ * NY + y_, "col": xl_ * NZ + z_}

    def remote(src, dst, s, rcv, to):
        return pltpu.make_async_remote_copy(
            src_ref=src, dst_ref=dst, send_sem=s, recv_sem=rcv, device_id=to, device_id_type=MESH
        )

    own = [
        pltpu.make_async_copy(tokens, tk.at[z], local.at[0]),
        pltpu.make_async_copy(weight, wg.at[z], local.at[1]),
        pltpu.make_async_copy(og, ogy.at[pl.ds(y * ob, ob)], local.at[2]),
    ]
    for o in own:
        o.start()

    barrier = pltpu.get_barrier_semaphore()
    peers = [dev(xh, lax.rem(y + k, NY), xl, z) for k in range(1, NY)]
    peers += [dev(xh, y, xl, lax.rem(z + k, NZ)) for k in range(1, NZ)]
    peers += [dev(1 - xh, y, xl, z), dev(xh, y, 1 - xl, z), dev(1 - xh, y, 1 - xl, z)]
    for p in peers:
        pl.semaphore_signal(barrier, inc=1, device_id=p, device_id_type=MESH)
    pl.semaphore_wait(barrier, len(peers))

    y_copies = []
    for k in range(1, NY):
        y_copies.append(
            remote(og, ogy.at[pl.ds(y * ob, ob)], y_send.at[k - 1], y_recv.at[k - 1], dev(xh, lax.rem(y + k, NY), xl, z))
        )
        y_copies[-1].start()

    right, left = lax.rem(z + 1, NZ), lax.rem(z + NZ - 1, NZ)

    def piece(item, src_z, half):
        d0, width = items[item]
        if item < n_chunks:
            rows = pl.ds(0, tb) if half is None else pl.ds(half * (tb // 2), tb // 2)
            return tk.at[src_z, rows, pl.ds(d0, width)]
        rows = pl.ds(d0, width) if half is None else pl.ds(d0 + half * (width // 2), width // 2)
        return wg.at[src_z, rows]

    def ring_copy(item, way, hop):
        half = way if hop == NZ // 2 else None
        step = hop - 1
        src_z = lax.rem(z + (NZ - step if way == 0 else step), NZ)
        ref = piece(item, src_z, half)
        src = ref
        to = right if way == 0 else left
        return remote(src, ref, ring_send.at[item, way, step], ring_recv.at[item, way, step], dev(xh, y, xl, to))

    def ring_arrival(item, way, hop):
        half = way if hop == NZ // 2 else None
        src_z = lax.rem(z + (NZ - hop if way == 0 else hop), NZ)
        ref = piece(item, src_z, half)
        return remote(ref, ref, ring_send.at[item, way, hop - 1], ring_recv.at[item, way, hop - 1], dev(xh, y, xl, right))

    own[0].wait()
    ring_copies = []

    def ring_start(item, hop, ways=(0, 1)):
        for way in ways:
            copy = ring_copy(item, way, hop)
            copy.start()
            ring_copies.append(copy)

    same = xh == xl

    def w_copy(k):
        return remote(og, ogw.at[xl, pl.ds(y * ob, ob)], w_send.at[k], w_recv.at[xl], dev(k, y, xh, z))

    def w_arrival(j):
        ref = ogw.at[j, pl.ds(y * ob, ob)]
        return remote(ref, ref, w_send.at[j], w_recv.at[j], dev(xh, y, 1 - xl, z))

    def w_local():
        return pltpu.make_async_copy(og, ogw.at[xl, pl.ds(y * ob, ob)], local.at[3])

    def w_start():
        for k in range(XH):
            @pl.when(jnp.logical_or(k != xh, jnp.logical_not(same)))
            def _():
                w_copy(k).start()

        @pl.when(same)
        def _():
            w_local().start()

    def w_wait():
        for j in range(XL):
            @pl.when(jnp.logical_or(j != xl, jnp.logical_not(same)))
            def _():
                w_arrival(j).wait_recv()

        @pl.when(same)
        def _():
            w_local().wait()

    def w_wait_send():
        for k in range(XH):
            @pl.when(jnp.logical_or(k != xh, jnp.logical_not(same)))
            def _():
                w_copy(k).wait_send()

    def v_copy(k):
        ref = ogw.at[:, pl.ds(y * ob, ob)]
        return remote(ref, ref, v_send.at[k - 1], v_recv.at[k - 1], dev(xh, lax.rem(y + k, NY), xl, z))

    def v_arrival(k):
        ref = ogw.at[:, pl.ds(lax.rem(y + NY - k, NY) * ob, ob)]
        return remote(ref, ref, v_send.at[k - 1], v_recv.at[k - 1], dev(xh, lax.rem(y + k, NY), xl, z))

    def strip(h, y_):
        return ogi.at[:, h, pl.ds(y_ * quarter, quarter)]

    def z_copy(k):
        to = lax.rem(z + k, NZ)
        src = ogy.at[pl.ds(to * tb + y * quarter, quarter)]
        return remote(src, ogi.at[z, xh, pl.ds(y * quarter, quarter)], z_send.at[k - 1], z_recv.at[k - 1], dev(xh, y, xl, to))

    def z_arrival(k):
        at = lax.rem(z + NZ - k, NZ)
        ref = ogi.at[at, xh, pl.ds(y * quarter, quarter)]
        return remote(ref, ref, z_send.at[k - 1], z_recv.at[k - 1], dev(xh, y, xl, at))

    z_local = pltpu.make_async_copy(
        ogy.at[pl.ds(z * tb + y * quarter, quarter)], ogi.at[z, xh, pl.ds(y * quarter, quarter)], local.at[4]
    )
    h_copy = remote(strip(xh, y), strip(xh, y), h_send, h_recv, dev(1 - xh, y, xl, z))
    h_arrival = remote(strip(1 - xh, y), strip(1 - xh, y), h_send, h_recv, dev(1 - xh, y, xl, z))

    def b_copy(which, k):
        h = xh if which == 0 else 1 - xh
        return remote(strip(h, y), strip(h, y), b_send.at[which, k - 1], b_recv.at[which, k - 1], dev(xh, lax.rem(y + k, NY), xl, z))

    def b_arrival(which, k):
        h = xh if which == 0 else 1 - xh
        ref = strip(h, lax.rem(y + NY - k, NY))
        return remote(ref, ref, b_send.at[which, k - 1], b_recv.at[which, k - 1], dev(xh, lax.rem(y + k, NY), xl, z))

    def x_copy(at):
        item, d0, width = prods[at]
        if item < n_chunks:
            src, dst = part.at[1 - xl, pl.ds(d0, width)], part_in.at[pl.ds(d0, width)]
        else:
            src, dst = quota.at[1 - xl, :, pl.ds(d0, width)], quota_in.at[:, pl.ds(d0, width)]
        return remote(src, dst, x_send.at[at], x_recv.at[at], dev(xh, y, 1 - xl, z))

    def multiply(at):
        item, d0, width = prods[at]
        if item < n_chunks:
            def body(i, _):
                cols = pl.ds(pl.multiple_of(d0 + i * 128, 128), 128)
                a = tk[:, :, cols].reshape(half_t, 128)
                for k in range(XL):
                    part[k, cols] = lax.dot_general(
                        a, ogw[k], (((0,), (0,)), ((), ())), preferred_element_type=jnp.float32
                    )
                return 0

            lax.fori_loop(0, width // 128, body, 0)
        else:
            def body(i, _):
                k = i
                total = jnp.zeros((tb, width), jnp.float32)
                for s in range(NZ):
                    total += lax.dot_general(
                        ogi[s, k], wg[s, pl.ds(d0, width)], (((1,), (1,)), ((), ())), preferred_element_type=jnp.float32
                    )
                quota[k, :, pl.ds(d0, width)] = total
                return 0

            lax.fori_loop(0, XL, body, 0)

    outs = []

    def finish(at):
        item, d0, width = prods[at]
        x_copy(at).wait_recv()
        if item < n_chunks:
            part[xl, pl.ds(d0, width)] = part[xl, pl.ds(d0, width)] + part_in[pl.ds(d0, width)]
            out = pltpu.make_async_copy(part.at[xl, pl.ds(d0, width)], wgrad_out.at[pl.ds(d0, width)], local.at[5 + at])
        else:
            cols = pl.ds(d0, width)
            in_grad[:, cols] = (quota[xl, :, cols] + quota_in[:, cols]).astype(in_grad.dtype)
            out = pltpu.make_async_copy(in_grad.at[:, cols], in_grad_out.at[:, cols], local.at[5 + at])
        out.start()
        outs.append(out)

    hops = NZ // 2
    waiting = []
    next_product = 0
    w_start()
    for item in range(LOOK):
        ring_start(item, 1)

    def due(item, hop):
        return min(item + PACE * (hop - 1), n_items - 1 + DRAIN + hop - 1)

    for step in range(due(n_items - 1, hops) + 1):
        for hop in range(hops, 0, -1):
            for item in [i for i in range(n_items) if due(i, hop) == step]:
                for way in (0, 1):
                    ring_arrival(item, way, hop).wait_recv()
                    if hop < hops:
                        ring_start(item, hop + 1, (way,))
        if step + LOOK < n_items:
            if step + LOOK == n_chunks:
                own[1].wait()
            ring_start(step + LOOK, 1)
        if step == STAGES[0]:
            own[2].wait()
            for k in range(1, NY):
                src = ogy.at[pl.ds(lax.rem(y + NY - k, NY) * ob, ob)]
                remote(src, src, y_send.at[k - 1], y_recv.at[k - 1], dev(xh, lax.rem(y + k, NY), xl, z)).wait_recv()
            w_wait()
            for k in range(1, NY):
                v_copy(k).start()
            for k in range(1, NZ):
                z_copy(k).start()
            z_local.start()
        if step == STAGES[1]:
            z_local.wait()
            for k in range(1, NZ):
                z_arrival(k).wait_recv()
            h_copy.start()
            for k in range(1, NY):
                b_copy(0, k).start()
        if step == STAGES[2]:
            h_arrival.wait_recv()
            for k in range(1, NY):
                b_copy(1, k).start()
        while next_product < len(prods) and due(prods[next_product][0], hops) <= step:
            if next_product == 0:
                for k in range(1, NY):
                    v_arrival(k).wait_recv()
            if next_product == n_chunks:
                for which in (0, 1):
                    for k in range(1, NY):
                        b_arrival(which, k).wait_recv()
            multiply(next_product)
            x_copy(next_product).start()
            waiting.append((step, next_product))
            next_product += 1
        while waiting and waiting[0][0] <= step - SETTLE:
            finish(waiting.pop(0)[1])
    for _, item in waiting:
        finish(item)

    for copy in y_copies + ring_copies:
        copy.wait_send()
    w_wait_send()
    for k in range(1, NY):
        v_copy(k).wait_send()
    for k in range(1, NZ):
        z_copy(k).wait_send()
    h_copy.wait_send()
    for which in (0, 1):
        for k in range(1, NY):
            b_copy(which, k).wait_send()
    for at in range(len(prods)):
        x_copy(at).wait_send()
    for out in outs:
        out.wait()


def products(tokens, out_grad, weight):
    tb, d = tokens.shape
    ob, f = out_grad.shape
    items = chunks()
    n_items, n_prods = len(items), len(parts_of(items))
    dma = pltpu.SemaphoreType.DMA
    flops = 4 * d * f * ob * XH * NY
    return pl.pallas_call(
        kernel,
        out_shape=(
            jax.ShapeDtypeStruct((d, f), jnp.float32),
            jax.ShapeDtypeStruct((tb, d), jnp.bfloat16),
        ),
        in_specs=[pl.BlockSpec(memory_space=pltpu.HBM)] * 3,
        out_specs=[pl.BlockSpec(memory_space=pl.ANY)] * 2,
        scratch_shapes=[
            pltpu.VMEM((NZ, tb, d), jnp.bfloat16),
            pltpu.VMEM((NZ, d, f), jnp.bfloat16),
            pltpu.VMEM((NY * ob, f), jnp.bfloat16),
            pltpu.VMEM((XL, NY * ob, f), jnp.bfloat16),
            pltpu.VMEM((NZ, XH, tb, f), jnp.bfloat16),
            pltpu.VMEM((XL, d, f), jnp.float32),
            pltpu.VMEM((d, f), jnp.float32),
            pltpu.VMEM((XL, tb, d), jnp.float32),
            pltpu.VMEM((tb, d), jnp.float32),
            pltpu.VMEM((tb, d), jnp.bfloat16),
            dma((n_items, 2, NZ // 2)),
            dma((n_items, 2, NZ // 2)),
            dma((NY - 1,)),
            dma((NY - 1,)),
            dma((XH,)),
            dma((XL,)),
            dma((NY - 1,)),
            dma((NY - 1,)),
            dma((NZ - 1,)),
            dma((NZ - 1,)),
            dma,
            dma,
            dma((2, NY - 1)),
            dma((2, NY - 1)),
            dma((n_prods,)),
            dma((n_prods,)),
            dma((5 + n_prods,)),
        ],
        compiler_params=pltpu.CompilerParams(
            collective_id=0, has_side_effects=True, vmem_limit_bytes=60 * 2**20
        ),
        cost_estimate=pl.CostEstimate(flops=flops, bytes_accessed=8 * 2**20, transcendentals=0),
    )(tokens, out_grad, weight)


def per_device(tokens, out_grad, weight, first_moment, second_moment):
    wgrad, in_grad = products(tokens, out_grad, weight)
    new_first = 0.9 * first_moment + 0.1 * wgrad
    new_second = 0.95 * second_moment + 0.05 * wgrad * wgrad
    first_hat = new_first / (1.0 - 0.9**ADAM_STEP)
    second_hat = new_second / (1.0 - 0.95**ADAM_STEP)
    old = weight.astype(jnp.float32)
    new_weight = (old - 0.001 * first_hat / (jnp.sqrt(second_hat) + 1e-08) - 0.0001 * old).astype(
        jnp.bfloat16
    )
    return (in_grad, new_weight, new_first, new_second)


def solution(mesh):
    placed = (
        P(("rep", "col"), "row"),
        P(("rep", "row"), "col"),
        P(("rep", "row"), "col"),
        P(("rep", "row"), "col"),
        P(("rep", "row"), "col"),
    )
    return jax.shard_map(
        per_device,
        mesh=mesh,
        in_specs=placed,
        out_specs=(
            P(("rep", "col"), "row"),
            P(("rep", "row"), "col"),
            P(("rep", "row"), "col"),
            P(("rep", "row"), "col"),
        ),
        check_vma=False,
    )
```

```python
import functools

import jax
import jax.numpy as jnp
from jax import lax
from jax.experimental import pallas as pl
from jax.experimental.pallas import tpu as pltpu
from jax.sharding import PartitionSpec as P

ADAM_STEP = 10
MESH = pl.DeviceIdType.MESH
XH, XL, NY, NZ = 2, 2, 4, 8
LOOK = 4
TOKEN_CHUNKS = (384, 384, 384, 384)
WEIGHT_CHUNKS = (512, 384, 384, 128, 128)
LAST = 128
PACE = 1
DRAIN = 0
SETTLE = 2
STAGES = (0, 1, 2)


def chunks():
    items = []
    for widths in (TOKEN_CHUNKS, WEIGHT_CHUNKS):
        first = 0
        for width in widths:
            items.append((first, width))
            first += width
    return items


def parts_of(items):
    parts = [(item, first, width) for item, (first, width) in enumerate(items[:-1])]
    first, width = items[-1]
    return parts + [(len(items) - 1, first + at, LAST) for at in range(0, width, LAST)]


def kernel(
    tokens, og, weight, wgrad_out, in_grad_out,
    tk, wg, ogy, ogw, ogi, part, part_in, quota, quota_in, in_grad,
    ring_send, ring_recv, y_send, y_recv, w_send, w_recv, v_send, v_recv, z_send, z_recv,
    h_send, h_recv, b_send, b_recv, x_send, x_recv, local,
):
    tb, d = tokens.shape
    ob, f = og.shape
    n_chunks, items = len(TOKEN_CHUNKS), chunks()
    n_items = len(items)
    prods = parts_of(items)
    quarter = tb // NY
    half_t = NZ * tb

    r, c = lax.axis_index("row"), lax.axis_index("col")
    xh, y = r // NY, lax.rem(r, NY)
    xl, z = c // NZ, lax.rem(c, NZ)

    def dev(xh_, y_, xl_, z_):
        return {"row": xh_ * NY + y_, "col": xl_ * NZ + z_}

    def remote(src, dst, s, rcv, to):
        return pltpu.make_async_remote_copy(
            src_ref=src, dst_ref=dst, send_sem=s, recv_sem=rcv, device_id=to, device_id_type=MESH
        )

    own = [
        pltpu.make_async_copy(tokens, tk.at[z], local.at[0]),
        pltpu.make_async_copy(weight, wg.at[z], local.at[1]),
        pltpu.make_async_copy(og, ogy.at[pl.ds(y * ob, ob)], local.at[2]),
    ]
    for o in own:
        o.start()

    barrier = pltpu.get_barrier_semaphore()
    peers = [dev(xh, lax.rem(y + k, NY), xl, z) for k in range(1, NY)]
    peers += [dev(xh, y, xl, lax.rem(z + k, NZ)) for k in range(1, NZ)]
    peers += [dev(1 - xh, y, xl, z), dev(xh, y, 1 - xl, z), dev(1 - xh, y, 1 - xl, z)]
    for p in peers:
        pl.semaphore_signal(barrier, inc=1, device_id=p, device_id_type=MESH)
    pl.semaphore_wait(barrier, len(peers))

    y_copies = []
    for k in range(1, NY):
        y_copies.append(
            remote(og, ogy.at[pl.ds(y * ob, ob)], y_send.at[k - 1], y_recv.at[k - 1], dev(xh, lax.rem(y + k, NY), xl, z))
        )
        y_copies[-1].start()

    right, left = lax.rem(z + 1, NZ), lax.rem(z + NZ - 1, NZ)

    def piece(item, src_z, half):
        d0, width = items[item]
        if item < n_chunks:
            rows = pl.ds(0, tb) if half is None else pl.ds(half * (tb // 2), tb // 2)
            return tk.at[src_z, rows, pl.ds(d0, width)]
        rows = pl.ds(d0, width) if half is None else pl.ds(d0 + half * (width // 2), width // 2)
        return wg.at[src_z, rows]

    def ring_copy(item, way, hop):
        half = way if hop == NZ // 2 else None
        step = hop - 1
        src_z = lax.rem(z + (NZ - step if way == 0 else step), NZ)
        ref = piece(item, src_z, half)
        src = ref
        to = right if way == 0 else left
        return remote(src, ref, ring_send.at[item, way, step], ring_recv.at[item, way, step], dev(xh, y, xl, to))

    def ring_arrival(item, way, hop):
        half = way if hop == NZ // 2 else None
        src_z = lax.rem(z + (NZ - hop if way == 0 else hop), NZ)
        ref = piece(item, src_z, half)
        return remote(ref, ref, ring_send.at[item, way, hop - 1], ring_recv.at[item, way, hop - 1], dev(xh, y, xl, right))

    own[0].wait()
    ring_copies = []

    def ring_start(item, hop, ways=(0, 1)):
        for way in ways:
            copy = ring_copy(item, way, hop)
            copy.start()
            ring_copies.append(copy)

    same = xh == xl

    def w_copy(k):
        return remote(og, ogw.at[xl, pl.ds(y * ob, ob)], w_send.at[k], w_recv.at[xl], dev(k, y, xh, z))

    def w_arrival(j):
        ref = ogw.at[j, pl.ds(y * ob, ob)]
        return remote(ref, ref, w_send.at[j], w_recv.at[j], dev(xh, y, 1 - xl, z))

    def w_local():
        return pltpu.make_async_copy(og, ogw.at[xl, pl.ds(y * ob, ob)], local.at[3])

    def w_start():
        for k in range(XH):
            @pl.when(jnp.logical_or(k != xh, jnp.logical_not(same)))
            def _():
                w_copy(k).start()

        @pl.when(same)
        def _():
            w_local().start()

    def w_wait():
        for j in range(XL):
            @pl.when(jnp.logical_or(j != xl, jnp.logical_not(same)))
            def _():
                w_arrival(j).wait_recv()

        @pl.when(same)
        def _():
            w_local().wait()

    def w_wait_send():
        for k in range(XH):
            @pl.when(jnp.logical_or(k != xh, jnp.logical_not(same)))
            def _():
                w_copy(k).wait_send()

    def v_copy(k):
        ref = ogw.at[:, pl.ds(y * ob, ob)]
        return remote(ref, ref, v_send.at[k - 1], v_recv.at[k - 1], dev(xh, lax.rem(y + k, NY), xl, z))

    def v_arrival(k):
        ref = ogw.at[:, pl.ds(lax.rem(y + NY - k, NY) * ob, ob)]
        return remote(ref, ref, v_send.at[k - 1], v_recv.at[k - 1], dev(xh, lax.rem(y + k, NY), xl, z))

    def strip(h, y_):
        return ogi.at[:, h, pl.ds(y_ * quarter, quarter)]

    def z_copy(k):
        to = lax.rem(z + k, NZ)
        src = ogy.at[pl.ds(to * tb + y * quarter, quarter)]
        return remote(src, ogi.at[z, xh, pl.ds(y * quarter, quarter)], z_send.at[k - 1], z_recv.at[k - 1], dev(xh, y, xl, to))

    def z_arrival(k):
        at = lax.rem(z + NZ - k, NZ)
        ref = ogi.at[at, xh, pl.ds(y * quarter, quarter)]
        return remote(ref, ref, z_send.at[k - 1], z_recv.at[k - 1], dev(xh, y, xl, at))

    z_local = pltpu.make_async_copy(
        ogy.at[pl.ds(z * tb + y * quarter, quarter)], ogi.at[z, xh, pl.ds(y * quarter, quarter)], local.at[4]
    )
    h_copy = remote(strip(xh, y), strip(xh, y), h_send, h_recv, dev(1 - xh, y, xl, z))
    h_arrival = remote(strip(1 - xh, y), strip(1 - xh, y), h_send, h_recv, dev(1 - xh, y, xl, z))

    def b_copy(which, k):
        h = xh if which == 0 else 1 - xh
        return remote(strip(h, y), strip(h, y), b_send.at[which, k - 1], b_recv.at[which, k - 1], dev(xh, lax.rem(y + k, NY), xl, z))

    def b_arrival(which, k):
        h = xh if which == 0 else 1 - xh
        ref = strip(h, lax.rem(y + NY - k, NY))
        return remote(ref, ref, b_send.at[which, k - 1], b_recv.at[which, k - 1], dev(xh, lax.rem(y + k, NY), xl, z))

    def x_copy(at):
        item, d0, width = prods[at]
        if item < n_chunks:
            src, dst = part.at[1 - xl, pl.ds(d0, width)], part_in.at[pl.ds(d0, width)]
        else:
            src, dst = quota.at[1 - xl, :, pl.ds(d0, width)], quota_in.at[:, pl.ds(d0, width)]
        return remote(src, dst, x_send.at[at], x_recv.at[at], dev(xh, y, 1 - xl, z))

    def multiply(at):
        item, d0, width = prods[at]
        if item < n_chunks:
            def body(i, _):
                cols = pl.ds(pl.multiple_of(d0 + i * 128, 128), 128)
                a = tk[:, :, cols].reshape(half_t, 128)
                for k in range(XL):
                    part[k, cols] = lax.dot_general(
                        a, ogw[k], (((0,), (0,)), ((), ())), preferred_element_type=jnp.float32
                    )
                return 0

            lax.fori_loop(0, width // 128, body, 0)
        else:
            def body(i, _):
                k = i
                total = jnp.zeros((tb, width), jnp.float32)
                for s in range(NZ):
                    total += lax.dot_general(
                        ogi[s, k], wg[s, pl.ds(d0, width)], (((1,), (1,)), ((), ())), preferred_element_type=jnp.float32
                    )
                quota[k, :, pl.ds(d0, width)] = total
                return 0

            lax.fori_loop(0, XL, body, 0)

    outs = []

    def finish(at):
        item, d0, width = prods[at]
        x_copy(at).wait_recv()
        if item < n_chunks:
            part[xl, pl.ds(d0, width)] = part[xl, pl.ds(d0, width)] + part_in[pl.ds(d0, width)]
            out = pltpu.make_async_copy(part.at[xl, pl.ds(d0, width)], wgrad_out.at[pl.ds(d0, width)], local.at[5 + at])
        else:
            cols = pl.ds(d0, width)
            in_grad[:, cols] = (quota[xl, :, cols] + quota_in[:, cols]).astype(in_grad.dtype)
            out = pltpu.make_async_copy(in_grad.at[:, cols], in_grad_out.at[:, cols], local.at[5 + at])
        out.start()
        outs.append(out)

    hops = NZ // 2
    waiting = []
    next_product = 0
    w_start()
    for item in range(LOOK):
        ring_start(item, 1)

    def due(item, hop):
        return min(item + PACE * (hop - 1), n_items - 1 + DRAIN + hop - 1)

    for step in range(due(n_items - 1, hops) + 1):
        for hop in range(hops, 0, -1):
            for item in [i for i in range(n_items) if due(i, hop) == step]:
                for way in (0, 1):
                    ring_arrival(item, way, hop).wait_recv()
                    if hop < hops:
                        ring_start(item, hop + 1, (way,))
        if step + LOOK < n_items:
            if step + LOOK == n_chunks:
                own[1].wait()
            ring_start(step + LOOK, 1)
        if step == STAGES[0]:
            own[2].wait()
            for k in range(1, NY):
                src = ogy.at[pl.ds(lax.rem(y + NY - k, NY) * ob, ob)]
                remote(src, src, y_send.at[k - 1], y_recv.at[k - 1], dev(xh, lax.rem(y + k, NY), xl, z)).wait_recv()
            w_wait()
            for k in range(1, NY):
                v_copy(k).start()
            for k in range(1, NZ):
                z_copy(k).start()
            z_local.start()
        if step == STAGES[1]:
            z_local.wait()
            for k in range(1, NZ):
                z_arrival(k).wait_recv()
            h_copy.start()
            for k in range(1, NY):
                b_copy(0, k).start()
        if step == STAGES[2]:
            h_arrival.wait_recv()
            for k in range(1, NY):
                b_copy(1, k).start()
        while next_product < len(prods) and due(prods[next_product][0], hops) <= step:
            if next_product == 0:
                for k in range(1, NY):
                    v_arrival(k).wait_recv()
            if next_product == n_chunks:
                for which in (0, 1):
                    for k in range(1, NY):
                        b_arrival(which, k).wait_recv()
            multiply(next_product)
            x_copy(next_product).start()
            waiting.append((step, next_product))
            next_product += 1
        while waiting and waiting[0][0] <= step - SETTLE:
            finish(waiting.pop(0)[1])
    for _, item in waiting:
        finish(item)

    for copy in y_copies + ring_copies:
        copy.wait_send()
    w_wait_send()
    for k in range(1, NY):
        v_copy(k).wait_send()
    for k in range(1, NZ):
        z_copy(k).wait_send()
    h_copy.wait_send()
    for which in (0, 1):
        for k in range(1, NY):
            b_copy(which, k).wait_send()
    for at in range(len(prods)):
        x_copy(at).wait_send()
    for out in outs:
        out.wait()


def products(tokens, out_grad, weight):
    tb, d = tokens.shape
    ob, f = out_grad.shape
    items = chunks()
    n_items, n_prods = len(items), len(parts_of(items))
    dma = pltpu.SemaphoreType.DMA
    flops = 4 * d * f * ob * XH * NY
    return pl.pallas_call(
        kernel,
        out_shape=(
            jax.ShapeDtypeStruct((d, f), jnp.float32),
            jax.ShapeDtypeStruct((tb, d), jnp.bfloat16),
        ),
        in_specs=[pl.BlockSpec(memory_space=pltpu.HBM)] * 3,
        out_specs=[pl.BlockSpec(memory_space=pl.ANY)] * 2,
        scratch_shapes=[
            pltpu.VMEM((NZ, tb, d), jnp.bfloat16),
            pltpu.VMEM((NZ, d, f), jnp.bfloat16),
            pltpu.VMEM((NY * ob, f), jnp.bfloat16),
            pltpu.VMEM((XL, NY * ob, f), jnp.bfloat16),
            pltpu.VMEM((NZ, XH, tb, f), jnp.bfloat16),
            pltpu.VMEM((XL, d, f), jnp.float32),
            pltpu.VMEM((d, f), jnp.float32),
            pltpu.VMEM((XL, tb, d), jnp.float32),
            pltpu.VMEM((tb, d), jnp.float32),
            pltpu.VMEM((tb, d), jnp.bfloat16),
            dma((n_items, 2, NZ // 2)),
            dma((n_items, 2, NZ // 2)),
            dma((NY - 1,)),
            dma((NY - 1,)),
            dma((XH,)),
            dma((XL,)),
            dma((NY - 1,)),
            dma((NY - 1,)),
            dma((NZ - 1,)),
            dma((NZ - 1,)),
            dma,
            dma,
            dma((2, NY - 1)),
            dma((2, NY - 1)),
            dma((n_prods,)),
            dma((n_prods,)),
            dma((5 + n_prods,)),
        ],
        compiler_params=pltpu.CompilerParams(
            collective_id=0, has_side_effects=True, vmem_limit_bytes=60 * 2**20
        ),
        cost_estimate=pl.CostEstimate(flops=flops, bytes_accessed=8 * 2**20, transcendentals=0),
    )(tokens, out_grad, weight)


def per_device(tokens, out_grad, weight, first_moment, second_moment):
    wgrad, in_grad = products(tokens, out_grad, weight)
    new_first = 0.9 * first_moment + 0.1 * wgrad
    new_second = 0.95 * second_moment + 0.05 * wgrad * wgrad
    first_hat = new_first / (1.0 - 0.9**ADAM_STEP)
    second_hat = new_second / (1.0 - 0.95**ADAM_STEP)
    old = weight.astype(jnp.float32)
    new_weight = (old - 0.001 * first_hat / (jnp.sqrt(second_hat) + 1e-08) - 0.0001 * old).astype(
        jnp.bfloat16
    )
    return (in_grad, new_weight, new_first, new_second)


def solution(mesh):
    placed = (
        P(("rep", "col"), "row"),
        P(("rep", "row"), "col"),
        P(("rep", "row"), "col"),
        P(("rep", "row"), "col"),
        P(("rep", "row"), "col"),
    )
    return jax.shard_map(
        per_device,
        mesh=mesh,
        in_specs=placed,
        out_specs=(
            P(("rep", "col"), "row"),
            P(("rep", "row"), "col"),
            P(("rep", "row"), "col"),
            P(("rep", "row"), "col"),
        ),
        check_vma=False,
    )
```
